512 devices in a mesh: dp: 8 (over x, z_lo), feat: 64 (over y, z_hi, core).
Axes of the slice: x: 4, y: 8, z: 8 (z_hi: 4, z_lo: 2; z = z_hi * 2 + z_lo), core: 2. Of those that a mesh axis runs over, the one named last changes fastest.
Arguments:
- tokens: bfloat16 [16384, 8192], P('dp', 'feat'), may hold values from -6 to 6
- up_factor: bfloat16 [64, 128, 512], P('feat'), may hold values from -0.5 to 0.5
- down_factor: bfloat16 [64, 512, 128], P('feat'), may hold values from -0.25 to 0.25
- grad_out: bfloat16 [16384, 8192], P('dp', 'feat'), may hold values from -6 to 6
Outputs:
- mixed: bfloat16 [16384, 8192], P('dp', 'feat')
- grad_in: bfloat16 [16384, 8192], P('dp', 'feat')
- up_grad: float32 [64, 128, 512], P('feat', 'dp')
- down_grad: float32 [64, 512, 128], P('feat', 'dp')
The draws below stay inside these ranges and needn't reach their ends.
All inputs are finite; a program needn't handle non-finite values.
Results may differ from the reference program's by a relative error of at most 0.0061.
Values may be sent and summed in bfloat16 or wider, within the bound.
A program may use at most 64 MiB of HBM per device.

```python
import jax
import jax.numpy as jnp
from jax import lax

D = 8192
BLOCKS = 64
BW = 128
HB = 512
TOK_DEV = 2048
TOKENS = 16384
N_DP = 8


def steps_of(stream_key, extent, shards, low, largest):
    level = 1.0
    for axis_at, parts in shards:
        heights = jax.random.uniform(jax.random.fold_in(jax.random.fold_in(stream_key, 6), axis_at), (parts,), jnp.float32, low / len(shards), largest / len(shards))
        level = level * jnp.repeat(jnp.exp(heights), extent[axis_at] // parts).reshape((-1,) + (1,) * (len(extent) - 1 - axis_at))
    return level


def noise(key, extent, scale, most, shards=(), held_as=jnp.bfloat16):
    drawn = jax.random.normal(key, extent, jnp.float32) * scale
    if len(shards) > 0:
        drawn = steps_of(key, extent, shards, -0.22, 0.18) * drawn
    return jnp.clip(drawn, min=-most, max=most).astype(held_as)


def setup_inputs(seed: int = 0) -> dict:
    keys = jax.random.split(jax.random.key(seed), 5)
    tokens = noise(keys[0], (TOKENS, D), 1.0, 6.0, ((0, 8), (1, 64)))
    up_factor = noise(keys[1], (BLOCKS, BW, HB), BW ** -0.5, 0.5, ((0, 64),))
    down_factor = noise(keys[2], (BLOCKS, HB, BW), HB ** -0.5, 0.25, ((0, 64),))
    grad_out = noise(keys[3], (TOKENS, D), 1.0, 6.0, ((0, 8), (1, 64)))
    return {"tokens": tokens, "up_factor": up_factor, "down_factor": down_factor, "grad_out": grad_out}


def gelu_value(values):
    return 0.5 * values * (1.0 + jax.scipy.special.erf(values * 0.7071067811865476))


def gelu_slope(values):
    return 0.5 * (1.0 + jax.scipy.special.erf(values * 0.7071067811865476)) + values * jnp.exp(-0.5 * values * values) * 0.3989422804014327


def reference(tokens, up_factor, down_factor, grad_out):
    stride = HB // BLOCKS
    up_full = up_factor.astype(jnp.float32)
    down_full = down_factor.astype(jnp.float32).reshape(BLOCKS, BLOCKS, stride, BW)

    def one_shard(carry, item):
        inputs, upstream = item
        count = inputs.shape[0]
        split_in = inputs.reshape(count, BLOCKS, BW).astype(jnp.float32)
        first = jnp.einsum("tbi,bih->tbh", split_in, up_full).astype(jnp.bfloat16)
        relayed = first.reshape(count, BLOCKS, BLOCKS, stride).transpose(0, 2, 1, 3)
        relayed_f = relayed.astype(jnp.float32)
        active = gelu_value(relayed_f).astype(jnp.bfloat16)
        active_f = active.astype(jnp.float32)
        mixed = jnp.einsum("tcbk,cbko->tco", active_f, down_full).astype(jnp.bfloat16).reshape(count, D)
        grad_split = upstream.reshape(count, BLOCKS, BW).astype(jnp.float32)
        backward = jnp.einsum("tco,cbko->tcbk", grad_split, down_full)
        pushed = (backward * gelu_slope(relayed_f)).astype(jnp.bfloat16)
        down_term = jnp.einsum("tcbk,tco->cbko", active_f, grad_split).reshape(BLOCKS, HB, BW)
        back_hidden = pushed.transpose(0, 2, 1, 3).reshape(count, BLOCKS, HB).astype(jnp.float32)
        up_term = jnp.einsum("tbi,tbh->bih", split_in, back_hidden)
        grad_in = jnp.einsum("tbh,bih->tbi", back_hidden, up_full).astype(jnp.bfloat16).reshape(count, D)
        return (carry[0] + up_term, carry[1] + down_term), (mixed, grad_in)

    start = (jnp.zeros((BLOCKS, BW, HB), jnp.float32), jnp.zeros((BLOCKS, HB, BW), jnp.float32))
    sums, outputs = lax.scan(one_shard, start, (tokens.reshape(N_DP, TOK_DEV, D), grad_out.reshape(N_DP, TOK_DEV, D)))
    mixed = outputs[0].reshape(TOKENS, D)
    grad_in = outputs[1].reshape(TOKENS, D)
    return mixed, grad_in, sums[0], sums[1]
```

```python
import jax
import jax.numpy as jnp
from jax import lax
from jax.experimental import pallas as pl
from jax.experimental.pallas import tpu as pltpu
from jax.sharding import PartitionSpec as P

CHUNKS = 8
MESH = pl.DeviceIdType.MESH
F32 = jnp.float32
BF16 = jnp.bfloat16


def gelu_parts(values):
    phi = 0.5 * (1.0 + lax.erf(values * 0.7071067811865476))
    slope = phi + values * jnp.exp(-0.5 * values * values) * 0.3989422804014327
    return values * phi, slope


def dot(a, b, dims):
    return lax.dot_general(a, b, (dims, ((), ())), preferred_element_type=F32)


NN = ((1,), (0,))
NT = ((1,), (1,))


def kernel(
    tok_hbm, up_hbm, down_hbm, g_hbm,
    mixed_hbm, gin_hbm, upg_ref, downg_ref,
    tok, up, down, g, up_t, down_t, mixed, gin,
    fsend, frecv, bsend, brecv, upg_t, upg, downg, urecv, drecv,
    in_sems, out_sems, fs_sems, fr_sems, bs_sems, br_sems, dp_sems,
):
    feats = frecv.shape[1]
    half = frecv.shape[3]
    rows = 2 * half
    dps = urecv.shape[0]
    hidden = up.shape[1]
    stride = hidden // feats
    me = lax.axis_index("feat")
    dp = lax.axis_index("dp")

    barrier = pltpu.get_barrier_semaphore()

    @pl.loop(1, feats)
    def _(i):
        pl.semaphore_signal(barrier, inc=1, device_id=(dp, (me + i) % feats), device_id_type=MESH)

    @pl.loop(1, dps)
    def _(i):
        pl.semaphore_signal(barrier, inc=1, device_id=((dp + i) % dps, me), device_id_type=MESH)

    loads = [
        pltpu.make_async_copy(src, dst, in_sems.at[i])
        for i, (src, dst) in enumerate(((tok_hbm, tok), (up_hbm, up), (down_hbm, down), (g_hbm, g)))
    ]
    for load in loads:
        load.start()
    for load in loads:
        load.wait()
    up_t[...] = up[...].T
    down_t[...] = down[...].T
    upg_t[...] = jnp.zeros_like(upg_t)
    downg[...] = jnp.zeros_like(downg)

    def join(wide):
        first = wide[:, :half].reshape(feats, stride, half)
        second = wide[:, half:].reshape(feats, stride, half)
        return jnp.concatenate([first, second], axis=1).astype(BF16)

    def part(pieces):
        first = pieces[:, :stride, :].reshape(hidden, half)
        second = pieces[:, stride:, :].reshape(hidden, half)
        return jnp.concatenate([first, second], axis=1)

    def token_rows(ch):
        return pl.ds(pl.multiple_of(ch * rows, rows), rows)

    def project(ch):
        fsend[ch] = join(dot(up_t[...], tok[token_rows(ch), :], NT))

    def spread(ch, send, recv, ssems, rsems):
        recv[ch, me] = send[ch, me]

        @pl.loop(1, feats)
        def _(i):
            to = (me + 27 * i) % feats
            pltpu.make_async_remote_copy(
                src_ref=send.at[ch, to],
                dst_ref=recv.at[ch, me],
                send_sem=ssems.at[ch],
                recv_sem=rsems.at[ch],
                device_id=(dp, to),
                device_id_type=MESH,
            ).start()

    def arrived(ch, buffer, sems):
        whole = buffer.at[ch, pl.ds(0, feats - 1)]
        pltpu.make_async_copy(whole, whole, sems.at[ch]).wait()

    project(0)
    pl.semaphore_wait(barrier, feats - 1 + dps - 1)
    spread(0, fsend, frecv, fs_sems, fr_sems)

    @pl.loop(1, CHUNKS)
    def _(ch):
        project(ch)
        spread(ch, fsend, frecv, fs_sems, fr_sems)

    @pl.loop(0, CHUNKS)
    def _(ch):
        arrived(ch, frecv, fr_sems)
        at = token_rows(ch)
        upstream = g[at, :]
        active, slope = gelu_parts(frecv[ch].astype(F32))
        active = part(active).astype(BF16)
        mixed[at, :] = dot(down_t[...], active, NN).T.astype(BF16)
        pltpu.make_async_copy(mixed.at[at], mixed_hbm.at[at], out_sems.at[0]).start()
        bsend[ch] = join(dot(down[...], upstream, NT) * part(slope))
        spread(ch, bsend, brecv, bs_sems, br_sems)
        downg[...] += dot(active, upstream, NN)

    def reduce_start(grad, recv, s):
        share = recv.shape[1]
        recv[dp] = grad[pl.ds(pl.multiple_of(dp * share, share), share), :]

        @pl.loop(1, dps)
        def _(i):
            to = (dp + i) % dps
            pltpu.make_async_remote_copy(
                src_ref=grad.at[pl.ds(pl.multiple_of(to * share, share), share)],
                dst_ref=recv.at[dp],
                send_sem=dp_sems.at[s],
                recv_sem=dp_sems.at[s + 1],
                device_id=(to, me),
                device_id_type=MESH,
            ).start()

    def reduce_wait(recv, s):
        whole = recv.at[pl.ds(0, dps - 1)]
        pltpu.make_async_copy(whole, whole, dp_sems.at[s]).wait()

    reduce_start(downg, drecv, 0)

    @pl.loop(0, CHUNKS)
    def _(ch):
        arrived(ch, brecv, br_sems)
        at = token_rows(ch)
        back = part(brecv[ch].astype(F32)).astype(BF16)
        upg_t[...] += dot(back, tok[at, :], NN)
        gin[at, :] = dot(up[...], back, NN).T.astype(BF16)
        pltpu.make_async_copy(gin.at[at], gin_hbm.at[at], out_sems.at[1]).start()

    upg[...] = upg_t[...].T
    reduce_start(upg, urecv, 2)
    reduce_wait(drecv, 1)
    downg_ref[0] = jnp.sum(drecv[...], axis=0)

    @pl.loop(0, CHUNKS)
    def _(ch):
        arrived(ch, fsend, fs_sems)
        arrived(ch, bsend, bs_sems)

    reduce_wait(drecv, 0)
    pltpu.make_async_copy(mixed, mixed_hbm, out_sems.at[0]).wait()
    pltpu.make_async_copy(gin, gin_hbm, out_sems.at[1]).wait()
    reduce_wait(urecv, 3)
    upg_ref[0] = jnp.sum(urecv[...], axis=0)
    reduce_wait(urecv, 2)


def solution(mesh):
    feats = mesh.shape["feat"]
    dps = mesh.shape["dp"]

    def local(tokens, up_factor, down_factor, grad_out):
        count, width = tokens.shape
        hidden = up_factor.shape[2]
        half = count // CHUNKS // 2
        piece = (CHUNKS, feats, 2 * (hidden // feats), half)
        anywhere = pl.BlockSpec(memory_space=pl.ANY)
        inside = pl.BlockSpec(memory_space=pltpu.VMEM)
        return pl.pallas_call(
            kernel,
            out_shape=(
                jax.ShapeDtypeStruct((count, width), BF16),
                jax.ShapeDtypeStruct((count, width), BF16),
                jax.ShapeDtypeStruct((1, width // dps, hidden), F32),
                jax.ShapeDtypeStruct((1, hidden // dps, width), F32),
            ),
            in_specs=[anywhere] * 4,
            out_specs=(anywhere, anywhere, inside, inside),
            scratch_shapes=[
                pltpu.VMEM((count, width), BF16),
                pltpu.VMEM((width, hidden), BF16),
                pltpu.VMEM((hidden, width), BF16),
                pltpu.VMEM((count, width), BF16),
                pltpu.VMEM((hidden, width), BF16),
                pltpu.VMEM((width, hidden), BF16),
                pltpu.VMEM((count, width), BF16),
                pltpu.VMEM((count, width), BF16),
                pltpu.VMEM(piece, BF16),
                pltpu.VMEM(piece, BF16),
                pltpu.VMEM(piece, BF16),
                pltpu.VMEM(piece, BF16),
                pltpu.VMEM((hidden, width), F32),
                pltpu.VMEM((width, hidden), F32),
                pltpu.VMEM((hidden, width), F32),
                pltpu.VMEM((dps, width // dps, hidden), F32),
                pltpu.VMEM((dps, hidden // dps, width), F32),
                pltpu.SemaphoreType.DMA((4,)),
                pltpu.SemaphoreType.DMA((2,)),
                pltpu.SemaphoreType.DMA((CHUNKS,)),
                pltpu.SemaphoreType.DMA((CHUNKS,)),
                pltpu.SemaphoreType.DMA((CHUNKS,)),
                pltpu.SemaphoreType.DMA((CHUNKS,)),
                pltpu.SemaphoreType.DMA((4,)),
            ],
            compiler_params=pltpu.CompilerParams(
                collective_id=0, has_side_effects=True, vmem_limit_bytes=40 * 1024 * 1024
            ),
        )(tokens, up_factor.reshape(width, hidden), down_factor.reshape(hidden, width), grad_out)

    return jax.shard_map(
        local,
        mesh=mesh,
        in_specs=(P("dp", "feat"), P("feat", None, None), P("feat", None, None), P("dp", "feat")),
        out_specs=(P("dp", "feat"), P("dp", "feat"), P("feat", "dp", None), P("feat", "dp", None)),
        check_vma=False,
    )
```

```python
import jax
import jax.numpy as jnp
from jax import lax
from jax.experimental import pallas as pl
from jax.experimental.pallas import tpu as pltpu
from jax.sharding import PartitionSpec as P

CHUNKS = 4
VMEM_BYTES = 56 * 1024 * 1024
SIDE = 8
MESH = pl.DeviceIdType.MESH
F32 = jnp.float32
BF16 = jnp.bfloat16


def gelu_parts(values):
    phi = 0.5 * (1.0 + lax.erf(values * 0.7071067811865476))
    slope = phi + values * jnp.exp(-0.5 * values * values) * 0.3989422804014327
    return values * phi, slope


def dot(a, b, dims):
    return lax.dot_general(a, b, (dims, ((), ())), preferred_element_type=F32)


NN = ((1,), (0,))
NT = ((1,), (1,))


def kernel(
    tok_hbm, up_hbm, down_hbm, g_hbm,
    mixed_hbm, gin_hbm, upg_hbm, downg_hbm,
    tok, up, down, g, up_t, down_t, mixed, gin, upg_own, downg_own,
    fsend, frecv, bsend, brecv, upg_t, upg, downg, urecv, drecv,
    in_sems, out_sems, entered, fs_sems, fr_sems, bs_sems, br_sems, dp_sems,
):
    feats = frecv.shape[1]
    half = frecv.shape[3]
    rows = 2 * half
    dps = urecv.shape[0]
    hidden = up.shape[1]
    stride = hidden // feats
    me = lax.axis_index("feat")
    dp = lax.axis_index("dp")

    row = me // SIDE
    col = me % SIDE
    barrier = pltpu.get_barrier_semaphore()

    loads = [
        pltpu.make_async_copy(src, dst, in_sems.at[i])
        for i, (src, dst) in enumerate(((tok_hbm, tok), (up_hbm, up), (down_hbm, down), (g_hbm, g)))
    ]
    for load in loads:
        load.start()

    def in_row(i):
        return row * SIDE + (col + i) % SIDE

    def in_column(i):
        return ((row + i) % SIDE) * SIDE + col

    @pl.loop(1, SIDE)
    def _(i):
        pl.semaphore_signal(barrier, inc=1, device_id=(dp, in_row(i)), device_id_type=MESH)
        pl.semaphore_signal(barrier, inc=1, device_id=(dp, in_column(i)), device_id_type=MESH)

    @pl.loop(1, dps)
    def _(i):
        pl.semaphore_signal(barrier, inc=1, device_id=((dp + i) % dps, me), device_id_type=MESH)

    for load in loads:
        load.wait()
    up_t[...] = up[...].T
    down_t[...] = down[...].T
    upg_t[...] = jnp.zeros_like(upg_t)
    downg[...] = jnp.zeros_like(downg)

    def join(wide):
        first = wide[:, :half].reshape(feats, stride, half)
        second = wide[:, half:].reshape(feats, stride, half)
        return jnp.concatenate([first, second], axis=1).astype(BF16)

    def part(pieces):
        first = pieces[:, :stride, :].reshape(hidden, half)
        second = pieces[:, stride:, :].reshape(hidden, half)
        return jnp.concatenate([first, second], axis=1)

    def token_rows(ch):
        return pl.ds(pl.multiple_of(ch * rows, rows), rows)

    def project(ch):
        fsend[ch] = join(dot(up_t[...], tok[token_rows(ch), :], NT))

    def push(ch, to, send, recv, ssems, rsems):
        pltpu.make_async_remote_copy(
            src_ref=send.at[ch, to],
            dst_ref=recv.at[ch, me],
            send_sem=ssems.at[ch],
            recv_sem=rsems.at[ch],
            device_id=(dp, to),
            device_id_type=MESH,
        ).start()

    def spread_lines(ch, *buffers):
        @pl.loop(1, SIDE)
        def _(i):
            push(ch, in_row(i), *buffers)
            push(ch, in_column(i), *buffers)

    def spread_rest(ch, *buffers):
        @pl.loop(0, (SIDE - 1) * (SIDE - 1))
        def _(i):
            k = (27 * i) % ((SIDE - 1) * (SIDE - 1))
            to_row = (row + 1 + k // (SIDE - 1)) % SIDE
            to_col = (col + 1 + k % (SIDE - 1)) % SIDE
            push(ch, to_row * SIDE + to_col, *buffers)

    def spread(ch, send, recv, *sems):
        recv[ch, me] = send[ch, me]
        spread_lines(ch, send, recv, *sems)
        spread_rest(ch, send, recv, *sems)

    def arrived(ch, buffer, sems):
        whole = buffer.at[ch, pl.ds(0, feats - 1)]
        pltpu.make_async_copy(whole, whole, sems.at[ch]).wait()

    project(0)
    pl.semaphore_wait(barrier, 2 * (SIDE - 1) + dps - 1)

    @pl.loop(1, SIDE)
    def _(i):
        pl.semaphore_signal(entered, inc=1, device_id=(dp, in_row(i)), device_id_type=MESH)

    forward = (fsend, frecv, fs_sems, fr_sems)
    spread_lines(0, *forward)

    @pl.loop(1, CHUNKS)
    def _(ch):
        project(ch)
        spread_lines(ch, *forward)

    pl.semaphore_wait(entered, SIDE - 1)

    @pl.loop(0, CHUNKS)
    def _(ch):
        frecv[ch, me] = fsend[ch, me]
        spread_rest(ch, *forward)

    @pl.loop(0, CHUNKS)
    def _(ch):
        arrived(ch, frecv, fr_sems)
        at = token_rows(ch)
        upstream = g[at, :]
        active, slope = gelu_parts(frecv[ch].astype(F32))
        active = part(active).astype(BF16)
        mixed[at, :] = dot(down_t[...], active, NN).T.astype(BF16)
        pltpu.make_async_copy(mixed.at[at], mixed_hbm.at[at], out_sems.at[0]).start()
        bsend[ch] = join(dot(down[...], upstream, NT) * part(slope))
        spread(ch, bsend, brecv, bs_sems, br_sems)
        downg[...] += dot(active, upstream, NN)

    def reduce_start(grad, recv, s):
        share = recv.shape[1]
        recv[dp] = grad[pl.ds(pl.multiple_of(dp * share, share), share), :]

        @pl.loop(1, dps)
        def _(i):
            to = (dp + i) % dps
            pltpu.make_async_remote_copy(
                src_ref=grad.at[pl.ds(pl.multiple_of(to * share, share), share)],
                dst_ref=recv.at[dp],
                send_sem=dp_sems.at[s],
                recv_sem=dp_sems.at[s + 1],
                device_id=(to, me),
                device_id_type=MESH,
            ).start()

    def reduce_wait(recv, s):
        whole = recv.at[pl.ds(0, dps - 1)]
        pltpu.make_async_copy(whole, whole, dp_sems.at[s]).wait()

    reduce_start(downg, drecv, 0)

    @pl.loop(0, CHUNKS)
    def _(ch):
        arrived(ch, brecv, br_sems)
        at = token_rows(ch)
        back = part(brecv[ch].astype(F32)).astype(BF16)
        upg_t[...] += dot(back, tok[at, :], NN)
        gin[at, :] = dot(up[...], back, NN).T.astype(BF16)
        pltpu.make_async_copy(gin.at[at], gin_hbm.at[at], out_sems.at[1]).start()

    upg[...] = upg_t[...].T
    reduce_start(upg, urecv, 2)
    reduce_wait(drecv, 1)
    downg_own[0] = jnp.sum(drecv[...], axis=0)
    down_out = pltpu.make_async_copy(downg_own, downg_hbm, out_sems.at[2])
    down_out.start()

    @pl.loop(0, CHUNKS)
    def _(ch):
        arrived(ch, fsend, fs_sems)
        arrived(ch, bsend, bs_sems)

    reduce_wait(drecv, 0)
    reduce_wait(urecv, 3)
    upg_own[0] = jnp.sum(urecv[...], axis=0)
    up_out = pltpu.make_async_copy(upg_own, upg_hbm, out_sems.at[3])
    up_out.start()
    pltpu.make_async_copy(mixed, mixed_hbm, out_sems.at[0]).wait()
    pltpu.make_async_copy(gin, gin_hbm, out_sems.at[1]).wait()
    down_out.wait()
    up_out.wait()
    reduce_wait(urecv, 2)


def hand_over(*refs):
    for i in range(4):
        refs[4 + i][...] = refs[i][...]


def solution(mesh):
    feats = mesh.shape["feat"]
    dps = mesh.shape["dp"]

    def local(tokens, up_factor, down_factor, grad_out):
        count, width = tokens.shape
        hidden = up_factor.shape[2]
        half = count // CHUNKS // 2
        piece = (CHUNKS, feats, 2 * (hidden // feats), half)
        outside = pl.BlockSpec(memory_space=pltpu.HBM)
        anywhere = pl.BlockSpec(memory_space=pl.ANY)
        results = (
            jax.ShapeDtypeStruct((count, width), BF16),
            jax.ShapeDtypeStruct((count, width), BF16),
            jax.ShapeDtypeStruct((1, width // dps, hidden), F32),
            jax.ShapeDtypeStruct((1, hidden // dps, width), F32),
        )
        held = pl.pallas_call(
            kernel,
            out_shape=results,
            in_specs=[outside] * 4,
            out_specs=(outside,) * 4,
            scratch_shapes=[
                pltpu.VMEM((count, width), BF16),
                pltpu.VMEM((width, hidden), BF16),
                pltpu.VMEM((hidden, width), BF16),
                pltpu.VMEM((count, width), BF16),
                pltpu.VMEM((hidden, width), BF16),
                pltpu.VMEM((width, hidden), BF16),
                pltpu.VMEM((count, width), BF16),
                pltpu.VMEM((count, width), BF16),
                pltpu.VMEM((1, width // dps, hidden), F32),
                pltpu.VMEM((1, hidden // dps, width), F32),
                pltpu.VMEM(piece, BF16),
                pltpu.VMEM(piece, BF16),
                pltpu.VMEM(piece, BF16),
                pltpu.VMEM(piece, BF16),
                pltpu.VMEM((hidden, width), F32),
                pltpu.VMEM((width, hidden), F32),
                pltpu.VMEM((hidden, width), F32),
                pltpu.VMEM((dps, width // dps, hidden), F32),
                pltpu.VMEM((dps, hidden // dps, width), F32),
                pltpu.SemaphoreType.DMA((4,)),
                pltpu.SemaphoreType.DMA((4,)),
                pltpu.SemaphoreType.REGULAR,
                pltpu.SemaphoreType.DMA((CHUNKS,)),
                pltpu.SemaphoreType.DMA((CHUNKS,)),
                pltpu.SemaphoreType.DMA((CHUNKS,)),
                pltpu.SemaphoreType.DMA((CHUNKS,)),
                pltpu.SemaphoreType.DMA((4,)),
            ],
            compiler_params=pltpu.CompilerParams(
                collective_id=0, has_side_effects=True, vmem_limit_bytes=VMEM_BYTES
            ),
        )(tokens, up_factor.reshape(width, hidden), down_factor.reshape(hidden, width), grad_out)
        return pl.pallas_call(
            hand_over,
            out_shape=results,
            in_specs=[pl.BlockSpec(memory_space=pltpu.VMEM)] * 4,
            out_specs=(pl.BlockSpec(memory_space=pltpu.VMEM),) * 4,
            compiler_params=pltpu.CompilerParams(vmem_limit_bytes=VMEM_BYTES),
        )(*held)

    return jax.shard_map(
        local,
        mesh=mesh,
        in_specs=(P("dp", "feat"), P("feat", None, None), P("feat", None, None), P("dp", "feat")),
        out_specs=(P("dp", "feat"), P("dp", "feat"), P("feat", "dp", None), P("feat", "dp", None)),
        check_vma=False,
    )
```

```python
import jax
import jax.numpy as jnp
from jax import lax
from jax.experimental import pallas as pl
from jax.experimental.pallas import tpu as pltpu
from jax.sharding import PartitionSpec as P

CHUNKS = 4
VMEM_BYTES = 56 * 1024 * 1024
SIDE = 8
MESH = pl.DeviceIdType.MESH
F32 = jnp.float32
BF16 = jnp.bfloat16


def gelu_parts(values):
    phi = 0.5 * (1.0 + lax.erf(values * 0.7071067811865476))
    slope = phi + values * jnp.exp(-0.5 * values * values) * 0.3989422804014327
    return values * phi, slope


def dot(a, b, dims):
    return lax.dot_general(a, b, (dims, ((), ())), preferred_element_type=F32)


NN = ((1,), (0,))
NT = ((1,), (1,))


def kernel(
    tok_hbm, up_hbm, down_hbm, g_hbm,
    mixed_hbm, gin_hbm, upg_hbm, downg_hbm,
    tok, up, down, g, up_t, down_t, mixed, gin, upg_own, downg_own,
    fsend, frecv, bsend, brecv, upg_t, upg, downg, urecv, drecv,
    in_sems, out_sems, entered, fs_sems, fr_sems, bs_sems, br_sems, dp_sems,
):
    feats = frecv.shape[1]
    half = frecv.shape[3]
    rows = 2 * half
    dps = urecv.shape[0]
    hidden = up.shape[1]
    stride = hidden // feats
    me = lax.axis_index("feat")
    dp = lax.axis_index("dp")

    row = me // SIDE
    col = me % SIDE
    barrier = pltpu.get_barrier_semaphore()

    loads = [
        pltpu.make_async_copy(src, dst, in_sems.at[i])
        for i, (src, dst) in enumerate(((tok_hbm, tok), (up_hbm, up), (down_hbm, down), (g_hbm, g)))
    ]
    for load in loads:
        load.start()

    def in_row(i):
        return row * SIDE + (col + i) % SIDE

    def in_column(i):
        return ((row + i) % SIDE) * SIDE + col

    @pl.loop(1, SIDE)
    def _(i):
        pl.semaphore_signal(barrier, inc=1, device_id=(dp, in_row(i)), device_id_type=MESH)
        pl.semaphore_signal(barrier, inc=1, device_id=(dp, in_column(i)), device_id_type=MESH)

    @pl.loop(1, dps)
    def _(i):
        pl.semaphore_signal(barrier, inc=1, device_id=((dp + i) % dps, me), device_id_type=MESH)

    loads[0].wait()
    loads[1].wait()
    up_t[...] = up[...].T

    def join(wide):
        first = wide[:, :half].reshape(feats, stride, half)
        second = wide[:, half:].reshape(feats, stride, half)
        return jnp.concatenate([first, second], axis=1).astype(BF16)

    def part(pieces):
        first = pieces[:, :stride, :].reshape(hidden, half)
        second = pieces[:, stride:, :].reshape(hidden, half)
        return jnp.concatenate([first, second], axis=1)

    def token_rows(ch):
        return pl.ds(pl.multiple_of(ch * rows, rows), rows)

    def project(ch):
        fsend[ch] = join(dot(up_t[...], tok[token_rows(ch), :], NT))

    def push(ch, to, send, recv, ssems, rsems):
        pltpu.make_async_remote_copy(
            src_ref=send.at[ch, to],
            dst_ref=recv.at[ch, me],
            send_sem=ssems.at[ch],
            recv_sem=rsems.at[ch],
            device_id=(dp, to),
            device_id_type=MESH,
        ).start()

    def spread_lines(ch, *buffers):
        @pl.loop(1, SIDE)
        def _(i):
            push(ch, in_row(i), *buffers)
            push(ch, in_column(i), *buffers)

    def spread_rest(ch, *buffers):
        @pl.loop(0, (SIDE - 1) * (SIDE - 1))
        def _(i):
            k = (27 * i) % ((SIDE - 1) * (SIDE - 1))
            to_row = (row + 1 + k // (SIDE - 1)) % SIDE
            to_col = (col + 1 + k % (SIDE - 1)) % SIDE
            push(ch, to_row * SIDE + to_col, *buffers)

    def spread(ch, send, recv, *sems):
        recv[ch, me] = send[ch, me]
        spread_lines(ch, send, recv, *sems)
        spread_rest(ch, send, recv, *sems)

    def arrived(ch, buffer, sems):
        whole = buffer.at[ch, pl.ds(0, feats - 1)]
        pltpu.make_async_copy(whole, whole, sems.at[ch]).wait()

    project(0)
    pl.semaphore_wait(barrier, 2 * (SIDE - 1) + dps - 1)

    forward = (fsend, frecv, fs_sems, fr_sems)
    spread_lines(0, *forward)

    @pl.loop(1, SIDE)
    def _(i):
        pl.semaphore_signal(entered, inc=1, device_id=(dp, in_row(i)), device_id_type=MESH)

    @pl.loop(1, CHUNKS)
    def _(ch):
        project(ch)
        spread_lines(ch, *forward)

    loads[2].wait()
    loads[3].wait()
    down_t[...] = down[...].T
    upg_t[...] = jnp.zeros_like(upg_t)
    downg[...] = jnp.zeros_like(downg)
    pl.semaphore_wait(entered, SIDE - 1)

    @pl.loop(0, CHUNKS)
    def _(ch):
        frecv[ch, me] = fsend[ch, me]
        spread_rest(ch, *forward)

    @pl.loop(0, CHUNKS)
    def _(ch):
        arrived(ch, frecv, fr_sems)
        at = token_rows(ch)
        upstream = g[at, :]
        active, slope = gelu_parts(frecv[ch].astype(F32))
        active = part(active).astype(BF16)
        mixed[at, :] = dot(down_t[...], active, NN).T.astype(BF16)
        pltpu.make_async_copy(mixed.at[at], mixed_hbm.at[at], out_sems.at[0]).start()
        bsend[ch] = join(dot(down[...], upstream, NT) * part(slope))
        spread(ch, bsend, brecv, bs_sems, br_sems)
        downg[...] += dot(active, upstream, NN)

    def reduce_start(grad, recv, s):
        share = recv.shape[1]
        recv[dp] = grad[pl.ds(pl.multiple_of(dp * share, share), share), :]

        @pl.loop(1, dps)
        def _(i):
            to = (dp + i) % dps
            pltpu.make_async_remote_copy(
                src_ref=grad.at[pl.ds(pl.multiple_of(to * share, share), share)],
                dst_ref=recv.at[dp],
                send_sem=dp_sems.at[s],
                recv_sem=dp_sems.at[s + 1],
                device_id=(to, me),
                device_id_type=MESH,
            ).start()

    def reduce_wait(recv, s):
        whole = recv.at[pl.ds(0, dps - 1)]
        pltpu.make_async_copy(whole, whole, dp_sems.at[s]).wait()

    reduce_start(downg, drecv, 0)

    def back_of(ch):
        arrived(ch, brecv, br_sems)
        back = part(brecv[ch].astype(F32)).astype(BF16)
        upg_t[...] += dot(back, tok[token_rows(ch), :], NN)
        return back

    def finish(ch, back):
        at = token_rows(ch)
        gin[at, :] = dot(up[...], back, NN).T.astype(BF16)
        pltpu.make_async_copy(gin.at[at], gin_hbm.at[at], out_sems.at[1]).start()

    @pl.loop(0, CHUNKS - 1)
    def _(ch):
        finish(ch, back_of(ch))

    last = back_of(CHUNKS - 1)
    upg[...] = upg_t[...].T
    reduce_start(upg, urecv, 2)
    finish(CHUNKS - 1, last)
    reduce_wait(drecv, 1)
    downg_own[0] = jnp.sum(drecv[...], axis=0)
    down_out = pltpu.make_async_copy(downg_own, downg_hbm, out_sems.at[2])
    down_out.start()

    @pl.loop(0, CHUNKS)
    def _(ch):
        arrived(ch, fsend, fs_sems)
        arrived(ch, bsend, bs_sems)

    reduce_wait(drecv, 0)
    reduce_wait(urecv, 3)
    upg_own[0] = jnp.sum(urecv[...], axis=0)
    up_out = pltpu.make_async_copy(upg_own, upg_hbm, out_sems.at[3])
    up_out.start()
    pltpu.make_async_copy(mixed, mixed_hbm, out_sems.at[0]).wait()
    pltpu.make_async_copy(gin, gin_hbm, out_sems.at[1]).wait()
    down_out.wait()
    up_out.wait()
    reduce_wait(urecv, 2)


def hand_over(*refs):
    for i in range(4):
        refs[4 + i][...] = refs[i][...]


def solution(mesh):
    feats = mesh.shape["feat"]
    dps = mesh.shape["dp"]

    def local(tokens, up_factor, down_factor, grad_out):
        count, width = tokens.shape
        hidden = up_factor.shape[2]
        half = count // CHUNKS // 2
        piece = (CHUNKS, feats, 2 * (hidden // feats), half)
        outside = pl.BlockSpec(memory_space=pltpu.HBM)
        anywhere = pl.BlockSpec(memory_space=pl.ANY)
        results = (
            jax.ShapeDtypeStruct((count, width), BF16),
            jax.ShapeDtypeStruct((count, width), BF16),
            jax.ShapeDtypeStruct((1, width // dps, hidden), F32),
            jax.ShapeDtypeStruct((1, hidden // dps, width), F32),
        )
        held = pl.pallas_call(
            kernel,
            out_shape=results,
            in_specs=[outside] * 4,
            out_specs=(outside,) * 4,
            scratch_shapes=[
                pltpu.VMEM((count, width), BF16),
                pltpu.VMEM((width, hidden), BF16),
                pltpu.VMEM((hidden, width), BF16),
                pltpu.VMEM((count, width), BF16),
                pltpu.VMEM((hidden, width), BF16),
                pltpu.VMEM((width, hidden), BF16),
                pltpu.VMEM((count, width), BF16),
                pltpu.VMEM((count, width), BF16),
                pltpu.VMEM((1, width // dps, hidden), F32),
                pltpu.VMEM((1, hidden // dps, width), F32),
                pltpu.VMEM(piece, BF16),
                pltpu.VMEM(piece, BF16),
                pltpu.VMEM(piece, BF16),
                pltpu.VMEM(piece, BF16),
                pltpu.VMEM((hidden, width), F32),
                pltpu.VMEM((width, hidden), F32),
                pltpu.VMEM((hidden, width), F32),
                pltpu.VMEM((dps, width // dps, hidden), F32),
                pltpu.VMEM((dps, hidden // dps, width), F32),
                pltpu.SemaphoreType.DMA((4,)),
                pltpu.SemaphoreType.DMA((4,)),
                pltpu.SemaphoreType.REGULAR,
                pltpu.SemaphoreType.DMA((CHUNKS,)),
                pltpu.SemaphoreType.DMA((CHUNKS,)),
                pltpu.SemaphoreType.DMA((CHUNKS,)),
                pltpu.SemaphoreType.DMA((CHUNKS,)),
                pltpu.SemaphoreType.DMA((4,)),
            ],
            compiler_params=pltpu.CompilerParams(
                collective_id=0, has_side_effects=True, vmem_limit_bytes=VMEM_BYTES
            ),
        )(tokens, up_factor.reshape(width, hidden), down_factor.reshape(hidden, width), grad_out)
        return pl.pallas_call(
            hand_over,
            out_shape=results,
            in_specs=[pl.BlockSpec(memory_space=pltpu.VMEM)] * 4,
            out_specs=(pl.BlockSpec(memory_space=pltpu.VMEM),) * 4,
            compiler_params=pltpu.CompilerParams(vmem_limit_bytes=VMEM_BYTES),
        )(*held)

    return jax.shard_map(
        local,
        mesh=mesh,
        in_specs=(P("dp", "feat"), P("feat", None, None), P("feat", None, None), P("dp", "feat")),
        out_specs=(P("dp", "feat"), P("dp", "feat"), P("feat", "dp", None), P("feat", "dp", None)),
        check_vma=False,
    )
```

```python
import jax
import jax.numpy as jnp
from jax import lax
from jax.experimental import pallas as pl
from jax.experimental.pallas import tpu as pltpu
from jax.sharding import PartitionSpec as P

CHUNKS = 4
VMEM_BYTES = 56 * 1024 * 1024
SIDE = 8
MESH = pl.DeviceIdType.MESH
F32 = jnp.float32
BF16 = jnp.bfloat16


def gelu_parts(values):
    phi = 0.5 * (1.0 + lax.erf(values * 0.7071067811865476))
    slope = phi + values * jnp.exp(-0.5 * values * values) * 0.3989422804014327
    return values * phi, slope


def dot(a, b, dims):
    return lax.dot_general(a, b, (dims, ((), ())), preferred_element_type=F32)


NN = ((1,), (0,))
NT = ((1,), (1,))


def kernel(
    tok_hbm, up_hbm, down_hbm, g_hbm,
    mixed_hbm, gin_hbm, urecv, downg_hbm,
    tok, up, down, g, up_t, down_t, mixed, gin, downg_own,
    fsend, frecv, bsend, brecv, upg_t, upg, downg, drecv,
    in_sems, out_sems, entered, fs_sems, fr_sems, bs_sems, br_sems, dp_sems, own_sems,
):
    feats = frecv.shape[1]
    half = frecv.shape[3]
    rows = 2 * half
    dps = drecv.shape[0]
    hidden = up.shape[1]
    stride = hidden // feats
    me = lax.axis_index("feat")
    dp = lax.axis_index("dp")

    row = me // SIDE
    col = me % SIDE
    barrier = pltpu.get_barrier_semaphore()

    loads = [
        pltpu.make_async_copy(src, dst, in_sems.at[i])
        for i, (src, dst) in enumerate(((tok_hbm, tok), (up_hbm, up), (down_hbm, down), (g_hbm, g)))
    ]
    for load in loads:
        load.start()

    def in_row(i):
        return row * SIDE + (col + i) % SIDE

    def in_column(i):
        return ((row + i) % SIDE) * SIDE + col

    @pl.loop(1, SIDE)
    def _(i):
        pl.semaphore_signal(barrier, inc=1, device_id=(dp, in_row(i)), device_id_type=MESH)
        pl.semaphore_signal(barrier, inc=1, device_id=(dp, in_column(i)), device_id_type=MESH)

    @pl.loop(1, dps)
    def _(i):
        pl.semaphore_signal(barrier, inc=1, device_id=((dp + i) % dps, me), device_id_type=MESH)

    loads[0].wait()
    loads[1].wait()
    up_t[...] = up[...].T

    def join(wide):
        first = wide[:, :half].reshape(feats, stride, half)
        second = wide[:, half:].reshape(feats, stride, half)
        return jnp.concatenate([first, second], axis=1).astype(BF16)

    def part(pieces):
        first = pieces[:, :stride, :].reshape(hidden, half)
        second = pieces[:, stride:, :].reshape(hidden, half)
        return jnp.concatenate([first, second], axis=1)

    def token_rows(ch):
        return pl.ds(pl.multiple_of(ch * rows, rows), rows)

    def project(ch):
        fsend[ch] = join(dot(up_t[...], tok[token_rows(ch), :], NT))

    def push(ch, to, send, recv, ssems, rsems):
        pltpu.make_async_remote_copy(
            src_ref=send.at[ch, to],
            dst_ref=recv.at[ch, me],
            send_sem=ssems.at[ch],
            recv_sem=rsems.at[ch],
            device_id=(dp, to),
            device_id_type=MESH,
        ).start()

    def spread_lines(ch, *buffers):
        @pl.loop(1, SIDE)
        def _(i):
            push(ch, in_row(i), *buffers)
            push(ch, in_column(i), *buffers)

    def spread_rest(ch, *buffers):
        @pl.loop(0, (SIDE - 1) * (SIDE - 1))
        def _(i):
            k = (27 * i) % ((SIDE - 1) * (SIDE - 1))
            to_row = (row + 1 + k // (SIDE - 1)) % SIDE
            to_col = (col + 1 + k % (SIDE - 1)) % SIDE
            push(ch, to_row * SIDE + to_col, *buffers)

    def spread(ch, send, recv, *sems):
        recv[ch, me] = send[ch, me]
        spread_lines(ch, send, recv, *sems)
        spread_rest(ch, send, recv, *sems)

    def arrived(ch, buffer, sems):
        whole = buffer.at[ch, pl.ds(0, feats - 1)]
        pltpu.make_async_copy(whole, whole, sems.at[ch]).wait()

    project(0)
    pl.semaphore_wait(barrier, 2 * (SIDE - 1) + dps - 1)

    forward = (fsend, frecv, fs_sems, fr_sems)
    spread_lines(0, *forward)

    @pl.loop(1, SIDE)
    def _(i):
        pl.semaphore_signal(entered, inc=1, device_id=(dp, in_row(i)), device_id_type=MESH)

    @pl.loop(1, CHUNKS)
    def _(ch):
        project(ch)
        spread_lines(ch, *forward)

    loads[2].wait()
    loads[3].wait()
    down_t[...] = down[...].T
    upg_t[...] = jnp.zeros_like(upg_t)
    downg[...] = jnp.zeros_like(downg)
    pl.semaphore_wait(entered, SIDE - 1)

    @pl.loop(0, CHUNKS)
    def _(ch):
        frecv[ch, me] = fsend[ch, me]
        spread_rest(ch, *forward)

    @pl.loop(0, CHUNKS)
    def _(ch):
        arrived(ch, frecv, fr_sems)
        at = token_rows(ch)
        upstream = g[at, :]
        active, slope = gelu_parts(frecv[ch].astype(F32))
        active = part(active).astype(BF16)
        mixed[at, :] = dot(down_t[...], active, NN).T.astype(BF16)
        pltpu.make_async_copy(mixed.at[at], mixed_hbm.at[at], out_sems.at[0]).start()
        bsend[ch] = join(dot(down[...], upstream, NT) * part(slope))
        spread(ch, bsend, brecv, bs_sems, br_sems)
        downg[...] += dot(active, upstream, NN)

    def reduce_start(grad, recv, s):
        share = recv.shape[1]
        own = grad.at[pl.ds(pl.multiple_of(dp * share, share), share)]
        pltpu.make_async_copy(own, recv.at[dp], own_sems.at[s // 2]).start()

        @pl.loop(1, dps)
        def _(i):
            to = (dp + i) % dps
            pltpu.make_async_remote_copy(
                src_ref=grad.at[pl.ds(pl.multiple_of(to * share, share), share)],
                dst_ref=recv.at[dp],
                send_sem=dp_sems.at[s],
                recv_sem=dp_sems.at[s + 1],
                device_id=(to, me),
                device_id_type=MESH,
            ).start()

    def own_wait(recv, s):
        pltpu.make_async_copy(recv.at[0], recv.at[0], own_sems.at[s]).wait()

    def reduce_wait(recv, s):
        whole = recv.at[pl.ds(0, dps - 1)]
        pltpu.make_async_copy(whole, whole, dp_sems.at[s]).wait()

    reduce_start(downg, drecv, 0)

    def back_of(ch):
        arrived(ch, brecv, br_sems)
        back = part(brecv[ch].astype(F32)).astype(BF16)
        upg_t[...] += dot(back, tok[token_rows(ch), :], NN)
        return back

    def finish(ch, back):
        at = token_rows(ch)
        gin[at, :] = dot(up[...], back, NN).T.astype(BF16)
        pltpu.make_async_copy(gin.at[at], gin_hbm.at[at], out_sems.at[1]).start()

    @pl.loop(0, CHUNKS - 1)
    def _(ch):
        finish(ch, back_of(ch))

    last = back_of(CHUNKS - 1)
    upg[...] = upg_t[...].T
    reduce_start(upg, urecv, 2)
    finish(CHUNKS - 1, last)
    reduce_wait(drecv, 1)
    own_wait(drecv, 0)
    downg_own[0] = jnp.sum(drecv[...], axis=0)
    down_out = pltpu.make_async_copy(downg_own, downg_hbm, out_sems.at[2])
    down_out.start()

    @pl.loop(0, CHUNKS)
    def _(ch):
        arrived(ch, fsend, fs_sems)
        arrived(ch, bsend, bs_sems)

    reduce_wait(drecv, 0)
    pltpu.make_async_copy(mixed, mixed_hbm, out_sems.at[0]).wait()
    pltpu.make_async_copy(gin, gin_hbm, out_sems.at[1]).wait()
    down_out.wait()
    own_wait(urecv, 1)
    reduce_wait(urecv, 3)
    reduce_wait(urecv, 2)


def hand_over(mixed, gin, up_terms, downg, mixed_out, gin_out, upg_out, downg_out):
    mixed_out[...] = mixed[...]
    gin_out[...] = gin[...]
    upg_out[0] = jnp.sum(up_terms[...], axis=0)
    downg_out[...] = downg[...]


def solution(mesh):
    feats = mesh.shape["feat"]
    dps = mesh.shape["dp"]

    def local(tokens, up_factor, down_factor, grad_out):
        count, width = tokens.shape
        hidden = up_factor.shape[2]
        half = count // CHUNKS // 2
        piece = (CHUNKS, feats, 2 * (hidden // feats), half)
        outside = pl.BlockSpec(memory_space=pltpu.HBM)
        anywhere = pl.BlockSpec(memory_space=pl.ANY)
        results = (
            jax.ShapeDtypeStruct((count, width), BF16),
            jax.ShapeDtypeStruct((count, width), BF16),
            jax.ShapeDtypeStruct((1, width // dps, hidden), F32),
            jax.ShapeDtypeStruct((1, hidden // dps, width), F32),
        )
        held = pl.pallas_call(
            kernel,
            out_shape=(
                results[0],
                results[1],
                jax.ShapeDtypeStruct((dps, width // dps, hidden), F32),
                results[3],
            ),
            in_specs=[outside] * 4,
            out_specs=(outside,) * 4,
            scratch_shapes=[
                pltpu.VMEM((count, width), BF16),
                pltpu.VMEM((width, hidden), BF16),
                pltpu.VMEM((hidden, width), BF16),
                pltpu.VMEM((count, width), BF16),
                pltpu.VMEM((hidden, width), BF16),
                pltpu.VMEM((width, hidden), BF16),
                pltpu.VMEM((count, width), BF16),
                pltpu.VMEM((count, width), BF16),
                pltpu.VMEM((1, hidden // dps, width), F32),
                pltpu.VMEM(piece, BF16),
                pltpu.VMEM(piece, BF16),
                pltpu.VMEM(piece, BF16),
                pltpu.VMEM(piece, BF16),
                pltpu.VMEM((hidden, width), F32),
                pltpu.VMEM((width, hidden), F32),
                pltpu.VMEM((hidden, width), F32),
                pltpu.VMEM((dps, hidden // dps, width), F32),
                pltpu.SemaphoreType.DMA((4,)),
                pltpu.SemaphoreType.DMA((4,)),
                pltpu.SemaphoreType.REGULAR,
                pltpu.SemaphoreType.DMA((CHUNKS,)),
                pltpu.SemaphoreType.DMA((CHUNKS,)),
                pltpu.SemaphoreType.DMA((CHUNKS,)),
                pltpu.SemaphoreType.DMA((CHUNKS,)),
                pltpu.SemaphoreType.DMA((4,)),
                pltpu.SemaphoreType.DMA((2,)),
            ],
            compiler_params=pltpu.CompilerParams(
                collective_id=0, has_side_effects=True, vmem_limit_bytes=VMEM_BYTES
            ),
        )(tokens, up_factor.reshape(width, hidden), down_factor.reshape(hidden, width), grad_out)
        return pl.pallas_call(
            hand_over,
            out_shape=results,
            in_specs=[pl.BlockSpec(memory_space=pltpu.VMEM)] * 4,
            out_specs=(pl.BlockSpec(memory_space=pltpu.VMEM),) * 4,
            compiler_params=pltpu.CompilerParams(vmem_limit_bytes=VMEM_BYTES),
        )(*held)

    return jax.shard_map(
        local,
        mesh=mesh,
        in_specs=(P("dp", "feat"), P("feat", None, None), P("feat", None, None), P("dp", "feat")),
        out_specs=(P("dp", "feat"), P("dp", "feat"), P("feat", "dp", None), P("feat", "dp", None)),
        check_vma=False,
    )
```
